256 devices in a mesh: shard: 32 (over y, z_lo, core), rep: 8 (over x, z_hi).
Axes of the slice: x: 4, y: 4, z: 8 (z_hi: 2, z_lo: 4; z = z_hi * 4 + z_lo), core: 2. Of those that a mesh axis runs over, the one named last changes fastest.
Arguments:
- table: float32 [524288, 256], P(('shard', 'rep')), may hold values from -6 to 6
- swap_mask: int32 [8], P('rep'), may hold values from 1 to 31
- swap_slots: int32 [256, 8], P(('shard', 'rep')), may hold values from 0 to 15, as said below
- hot_ids: int32 [32, 4], P('shard'), may hold values from 0 to 127, as said below
- req_idx: int32 [32, 2048, 16], P('shard'), may hold values from 0 to 16383
- req_count: int32 [32, 2048], P('shard'), may hold values from 1 to 16
Outputs:
- table_after: float32 [524288, 256], P(('shard', 'rep'))
- hot_cache: float32 [32, 512, 256], P('shard')
- pooled: float32 [32, 2048, 256], P('shard', 'rep')
The draws below stay inside these ranges and needn't reach their ends.
Inputs may be any that keep to these rules, and one draw needn't show every extreme that they name: `swap_slots`: the entries of a row are distinct local block numbers. `hot_ids`: the entries of a row are distinct block numbers of the group.
All inputs are finite; a program needn't handle non-finite values.
Results may differ from the reference program's by a relative error of at most 0.0003.
Values sent between devices are 32-bit elements; how exact they have to be, the bound alone decides.
No kernel may reach another device: no remote copies, remote signals or barrier semaphores. Data moves between devices by JAX's collectives and lax.ppermute only.
A program may use at most 64 MiB of HBM per device.

```python
import jax
import jax.numpy as jnp
from jax import lax

E = 256
BLOCK = 128
BLK_DEV = 16
SWAPS = 8
HOT = 4
K = 16
GROUP_BLOCKS = 128
GROUP_ROWS = 16384
ROWS = 524288
GROUP_REQ = 2048
N_SHARD = 32
N_REP = 8


def distinct_rows(key, row_total, choices_from, taken):
    row_keys = jax.random.split(key, row_total)
    return jax.vmap(lambda single: jax.random.permutation(single, choices_from)[:taken])(row_keys).astype(jnp.int32)


def draw_swap_slots(key, part):
    key = jax.random.fold_in(key, 11)
    return distinct_rows(key, N_SHARD * N_REP, BLK_DEV, SWAPS)


def draw_hot_ids(key, part):
    key = jax.random.fold_in(key, 23)
    return distinct_rows(key, N_SHARD, GROUP_BLOCKS, HOT)


def set_ends(values, stream_key, smallest, high):
    dims = values.shape
    spot = [jax.random.randint(jax.random.fold_in(stream_key, axis), (), 0, dims[axis]) for axis in range(len(dims))]
    values = values.at[tuple(spot)].set(smallest)
    longest = dims.index(max(dims))
    spot[longest] = (spot[longest] + 1) % dims[longest]
    return values.at[tuple(spot)].set(high)


def block_levels(own_key, extent, shards, low, high):
    level = 1.0
    for position, parts in shards:
        heights = jax.random.uniform(jax.random.fold_in(jax.random.fold_in(own_key, 6), position), (parts,), jnp.float32, low / len(shards), high / len(shards))
        level = level * jnp.repeat(jnp.exp(heights), extent[position] // parts).reshape((-1,) + (1,) * (len(extent) - 1 - position))
    return level


def bell_draw(rng, shape, width, bound, shards=(), kind=jnp.bfloat16):
    entries = jax.random.normal(rng, shape, jnp.float32) * width
    if len(shards) > 0:
        entries = block_levels(rng, shape, shards, -0.22, 0.18) * entries
    return jnp.clip(entries, min=-bound, max=bound).astype(kind)


def setup_inputs(seed: int = 0) -> dict:
    key_list = jax.random.split(jax.random.key(seed), 7)
    return {
        "table": bell_draw(key_list[0], (ROWS, E), 1.0, 6.0, ((0, 256),), jnp.float32),
        "swap_mask": set_ends(jax.random.randint(key_list[1], (N_REP,), 1, N_SHARD), jax.random.fold_in(key_list[1], 1), 1, N_SHARD - 1).astype(jnp.int32),
        "swap_slots": draw_swap_slots(jax.random.fold_in(key_list[6], 71), 0),
        "hot_ids": draw_hot_ids(jax.random.fold_in(key_list[6], 71), 0),
        "req_idx": set_ends(jax.random.randint(key_list[4], (N_SHARD, GROUP_REQ, K), 0, GROUP_ROWS), jax.random.fold_in(key_list[4], 1), 0, GROUP_ROWS - 1).astype(jnp.int32),
        "req_count": set_ends(jax.random.randint(key_list[5], (N_SHARD, GROUP_REQ), 1, K + 1), jax.random.fold_in(key_list[5], 1), 1, K).astype(jnp.int32),
    }


def pool_group(operands):
    group_table, index_rows, live_count = operands
    picked = group_table[index_rows]
    live_mask = jnp.arange(K, dtype=jnp.int32)[None, :] < live_count[:, None]
    summed = jnp.sum(jnp.where(live_mask[:, :, None], picked, jnp.float32(0.0)), axis=1)
    return summed / live_count[:, None].astype(jnp.float32)


def reference(table, swap_mask, swap_slots, hot_ids, req_idx, req_count):
    blocks = table.reshape(N_SHARD, N_REP, BLK_DEV, BLOCK, E)
    out_slots = swap_slots.reshape(N_SHARD, N_REP, SWAPS)
    shard_ids = jnp.arange(N_SHARD, dtype=jnp.int32)[:, None]
    rep_ids = jnp.arange(N_REP, dtype=jnp.int32)[None, :]
    partner = jnp.bitwise_xor(shard_ids, swap_mask[None, :].astype(jnp.int32))
    rep_full = jnp.broadcast_to(rep_ids, (N_SHARD, N_REP))
    source_slots = out_slots[partner, rep_full]
    incoming = blocks[partner[:, :, None], rep_full[:, :, None], source_slots]
    shard_full = jnp.broadcast_to(shard_ids, (N_SHARD, N_REP))
    swapped = blocks.at[shard_full[:, :, None], rep_full[:, :, None], out_slots].set(incoming)
    table_after = swapped.reshape(ROWS, E)
    groups = swapped.reshape(N_SHARD, GROUP_BLOCKS, BLOCK, E)
    hot_cache = jnp.take_along_axis(groups, hot_ids[:, :, None, None], axis=1).reshape(N_SHARD, HOT * BLOCK, E)
    pooled = lax.map(pool_group, (groups.reshape(N_SHARD, GROUP_ROWS, E), req_idx, req_count))
    return table_after, hot_cache, pooled
```

```python
import functools

import jax
import jax.numpy as jnp
from jax import lax
from jax.experimental import pallas as pl
from jax.experimental.pallas import tpu as pltpu
from jax.sharding import PartitionSpec as P

BLOCK = 128
E = 256
BLK_DEV = 16
SWAPS = 8
HOT = 4
K = 16
N_SHARD = 32
N_X = 4
N_REP = 8
OWN = 256
REQS = OWN * N_REP
PIECES = 8
HALF_ROWS = SWAPS * BLOCK
CHUNKS = 4
WIDE = E // CHUNKS
COUNT_INT = jnp.int16

SMEM = pl.BlockSpec(memory_space=pltpu.SMEM)
VMEM = pl.BlockSpec(memory_space=pltpu.VMEM)
ANY = pl.BlockSpec(memory_space=pl.ANY)


def f32(*shape):
    return jax.ShapeDtypeStruct(shape, jnp.float32)


def params(mib):
    return pltpu.CompilerParams(vmem_limit_bytes=mib * 2**20)


def cost(flops, moved):
    return pl.CostEstimate(flops=flops, bytes_accessed=moved, transcendentals=0)


def piece_owner(piece, rep):
    ahead = piece % N_X
    side = 1 - piece // N_X
    x = lax.rem(rep // 2 + ahead, N_X)
    return x * 2 + lax.rem(lax.rem(rep, 2) + side, 2)


def outgoing_kernel(slots, table, out, sems):
    copies = [
        pltpu.make_async_copy(table.at[slots[0, j]], out.at[j], sems.at[j]) for j in range(SWAPS)
    ]
    for copy in copies:
        copy.start()
    for copy in copies:
        copy.wait()


def outgoing(slots, blocks):
    return pl.pallas_call(
        outgoing_kernel,
        out_shape=f32(SWAPS, BLOCK, E),
        in_specs=[SMEM, ANY],
        out_specs=ANY,
        scratch_shapes=[pltpu.SemaphoreType.DMA((SWAPS,))],
        cost_estimate=cost(0, 2**21),
    )(slots, blocks)


def early_kernel(slots, raw_keys, counts, table, sums, later, keys, flags, order, parts):
    rep = lax.axis_index("rep")

    def clear(b, carry):
        flags[b] = 0
        return carry

    def mark(j, carry):
        flags[slots[0, j]] = 1
        order[SWAPS + j] = slots[0, j]
        return carry

    def list_block(b, found):
        @pl.when(flags[b] == 0)
        def _():
            order[found] = b

        return found + 1 - flags[b]

    lax.fori_loop(0, BLK_DEV, clear, 0)
    lax.fori_loop(0, SWAPS, mark, 0)
    lax.fori_loop(0, BLK_DEV, list_block, 0)
    live = lax.broadcasted_iota(jnp.int32, (K, REQS), 0) < counts[...]
    keys[...] = jnp.where(live, raw_keys[...], -1)

    def split(j, carry):
        put_parts(table[order[j]], j, parts)
        return carry

    lax.fori_loop(0, SWAPS, split, 0)
    row_in_tile = lax.broadcasted_iota(jnp.int32, (16, 128), 0).astype(COUNT_INT)
    one, zero = jnp.bfloat16(1), jnp.bfloat16(0)

    def one_piece(piece, carry):
        start = piece_owner(piece, rep) * OWN

        def one_block(step, inner):
            j = step // 2
            side = step % 2 * 128
            lanes = pl.multiple_of(start + side, 128)
            column = pl.multiple_of(side, 128)
            place = jnp.where(j < SWAPS, PIECES, piece)
            first = (rep * BLK_DEV + order[j]) * BLOCK
            near = []
            for k in range(K):
                offset = jnp.clip(keys[pl.ds(k, 1), pl.ds(lanes, 128)] - first, -1, BLOCK)
                near.append(jnp.broadcast_to(offset, (16, 128)).astype(COUNT_INT))
            for tile in range(BLOCK // 16):
                row = row_in_tile + jnp.array(tile * 16, COUNT_INT)
                total = jnp.where(near[0] == row, one, zero)
                for k in range(1, K):
                    total = total + jnp.where(near[k] == row, one, zero)
                row0 = pl.multiple_of(j % SWAPS * BLOCK + tile * 16, 16)
                later[place, pl.ds(row0, 16), pl.ds(column, 128)] = total
            return inner

        lax.fori_loop(0, BLK_DEV * 2, one_block, 0)
        apply_counts(parts, later.at[PIECES], sums.at[piece], None)
        return carry

    lax.fori_loop(0, PIECES, one_piece, 0)


def put_parts(rows, j, parts):
    turned = rows.T
    high = turned.astype(jnp.bfloat16)
    low = (turned - high.astype(jnp.float32)).astype(jnp.bfloat16)
    at = pl.ds(pl.multiple_of(j * BLOCK, BLOCK), BLOCK)
    for chunk in range(CHUNKS):
        parts[chunk, :WIDE, at] = high[chunk * WIDE : (chunk + 1) * WIDE]
        parts[chunk, WIDE:, at] = low[chunk * WIDE : (chunk + 1) * WIDE]


def apply_counts(parts, counted, out, base):
    def one_chunk(chunk, carry):
        both = jnp.dot(parts[chunk], counted[...], preferred_element_type=jnp.float32)
        total = both[:WIDE] + both[WIDE:]
        at = pl.ds(pl.multiple_of(chunk * WIDE, WIDE), WIDE)
        out[at] = total if base is None else total + base[at]
        return carry

    lax.fori_loop(0, CHUNKS, one_chunk, 0)


def early(slots, keys, counts, blocks):
    return pl.pallas_call(
        early_kernel,
        out_shape=(
            f32(PIECES, E, OWN),
            jax.ShapeDtypeStruct((PIECES + 1, HALF_ROWS, OWN), jnp.bfloat16),
        ),
        in_specs=[SMEM, VMEM, VMEM, VMEM],
        out_specs=(VMEM, VMEM),
        scratch_shapes=[
            pltpu.VMEM((K, REQS), jnp.int32),
            pltpu.SMEM((BLK_DEV,), jnp.int32),
            pltpu.SMEM((BLK_DEV,), jnp.int32),
            pltpu.VMEM((CHUNKS, 2 * WIDE, HALF_ROWS), jnp.bfloat16),
        ],
        compiler_params=params(32),
        cost_estimate=cost(2**34, 2**25),
    )(slots, keys, counts, blocks)


def late_kernel(sums, later, incoming, out0, out1, out2, out3, parts):
    def split(j, carry):
        put_parts(incoming[j], j, parts)
        return carry

    lax.fori_loop(0, SWAPS, split, 0)
    for ahead, out in ((2, out2), (1, out1), (3, out3), (0, out0)):
        apply_counts(parts, later.at[ahead], out, sums.at[ahead])


def late(first, sums, later, incoming):
    half = lambda *tail: pl.BlockSpec((N_X, *tail), lambda i: (first // N_X, 0, 0))
    whole = pl.BlockSpec((SWAPS, BLOCK, E), lambda i: (0, 0, 0))
    result = pl.BlockSpec((E, OWN), lambda i: (0, 0))
    return pl.pallas_call(
        late_kernel,
        grid=(1,),
        out_shape=(f32(E, OWN),) * N_X,
        in_specs=[half(E, OWN), half(HALF_ROWS, OWN), whole],
        out_specs=(result,) * N_X,
        scratch_shapes=[pltpu.VMEM((CHUNKS, 2 * WIDE, HALF_ROWS), jnp.bfloat16)],
        compiler_params=params(24),
        cost_estimate=cost(2**30, 2**22),
    )(sums, later, incoming)


def hot_first_kernel(slots, hot, table, incoming, *outs):
    rep = lax.axis_index("rep")
    for ahead, out in enumerate(outs):
        block = lax.rem(hot[0, lax.rem(rep // 2 + ahead, N_X)], BLK_DEV)
        came = jnp.int32(-1)
        for j in range(SWAPS):
            came = jnp.where(slots[0, j] == block, j, came)

        @pl.when(came >= 0)
        def _():
            out[...] = incoming[jnp.maximum(came, 0)]

        @pl.when(came < 0)
        def _():
            out[...] = table[block]


def hot_first(slots, hot, blocks, incoming):
    return pl.pallas_call(
        hot_first_kernel,
        out_shape=(f32(BLOCK, E),) * N_X,
        in_specs=[SMEM, SMEM, VMEM, VMEM],
        out_specs=(VMEM,) * N_X,
        compiler_params=params(16),
        cost_estimate=cost(0, 2**20),
    )(slots, hot, blocks, incoming)


def hot_pick_kernel(hot, in0, in1, in2, in3, out):
    x = lax.axis_index("rep") // 2
    owner_x = hot[0, x] // (2 * BLK_DEV)
    behind = lax.rem(x - owner_x + N_X, N_X)
    for back, source in enumerate((in0, in1, in2, in3)):

        @pl.when(behind == back)
        def _():
            out[...] = source[...]


def hot_pick(hot, pieces):
    return pl.pallas_call(
        hot_pick_kernel,
        out_shape=f32(BLOCK, E),
        in_specs=[SMEM] + [VMEM] * N_X,
        out_specs=VMEM,
        compiler_params=params(8),
        cost_estimate=cost(0, 2**18),
    )(hot, *pieces)


def hot_side_kernel(hot, mine, other, out):
    rep = lax.axis_index("rep")
    side = lax.rem(hot[0, rep // 2] // BLK_DEV, 2)

    @pl.when(side == lax.rem(rep, 2))
    def _():
        out[...] = mine[...]

    @pl.when(side != lax.rem(rep, 2))
    def _():
        out[...] = other[...]


def hot_side(hot, mine, other):
    return pl.pallas_call(
        hot_side_kernel,
        out_shape=f32(BLOCK, E),
        in_specs=[SMEM, VMEM, VMEM],
        out_specs=VMEM,
        compiler_params=params(8),
        cost_estimate=cost(0, 2**18),
    )(hot, mine, other)


def hot_last_kernel(in0, in1, in2, in3, out, sems):
    x = lax.axis_index("rep") // 2
    copies = [
        pltpu.make_async_copy(source, out.at[lax.rem(x - back + N_X, N_X)], sems.at[back])
        for back, source in enumerate((in0, in1, in2, in3))
    ]
    for copy in copies:
        copy.start()
    for copy in copies:
        copy.wait()


def hot_last(pieces):
    return pl.pallas_call(
        hot_last_kernel,
        out_shape=f32(HOT, BLOCK, E),
        in_specs=[VMEM] * N_X,
        out_specs=ANY,
        scratch_shapes=[pltpu.SemaphoreType.DMA((N_X,))],
        compiler_params=params(8),
        cost_estimate=cost(0, 2**20),
    )(*pieces)


def table_kernel(slots, table, incoming, out, came, sems):
    for b in range(BLK_DEV):
        came[b] = -1
    for j in range(SWAPS):
        came[slots[0, j]] = j
    for b in range(BLK_DEV):

        @pl.when(came[b] >= 0)
        def _():
            pltpu.make_async_copy(incoming.at[jnp.maximum(came[b], 0)], out.at[b], sems.at[b]).start()

        @pl.when(came[b] < 0)
        def _():
            pltpu.make_async_copy(table.at[b], out.at[b], sems.at[b]).start()

    for b in range(BLK_DEV):
        pltpu.make_async_copy(table.at[b], out.at[b], sems.at[b]).wait()


def table_after(slots, blocks, incoming):
    return pl.pallas_call(
        table_kernel,
        out_shape=f32(BLK_DEV, BLOCK, E),
        in_specs=[SMEM, VMEM, VMEM],
        out_specs=ANY,
        scratch_shapes=[pltpu.SMEM((BLK_DEV,), jnp.int32), pltpu.SemaphoreType.DMA((BLK_DEV,))],
        compiler_params=params(16),
        cost_estimate=cost(0, 2**22),
    )(slots, blocks, incoming)


def finish_kernel(counts, in0, in1, in2, in3, other, out):
    start = pl.multiple_of(lax.axis_index("rep") * OWN, OWN)
    total = in0[...] + in1[...] + in2[...] + in3[...] + other[...]
    mean = total / counts[:, pl.ds(start, OWN)].astype(jnp.float32)
    out[...] = mean.T


def finish(counts, pieces, other):
    return pl.pallas_call(
        finish_kernel,
        out_shape=f32(OWN, E),
        in_specs=[VMEM] * 6,
        out_specs=VMEM,
        compiler_params=params(16),
        cost_estimate=cost(2**19, 2**21),
    )(counts, *pieces, other)


def ahead_by(step):
    return [(x * 2 + z, (x + step) % N_X * 2 + z) for x in range(N_X) for z in range(2)]


def to_all_x(pieces):
    return [pieces[0]] + [lax.ppermute(pieces[n], "rep", ahead_by(n)) for n in range(1, N_X)]


def other_side(value):
    return lax.ppermute(value, "rep", [(r, r ^ 1) for r in range(N_REP)])


def body(table, swap_mask, swap_slots, hot_ids, req_idx, req_count):
    blocks = table.reshape(BLK_DEV, BLOCK, E)
    keys = req_idx[0].T
    leaving = outgoing(swap_slots, blocks)

    def branch(mask, operands):
        leaving, slots, keys, counts, blocks = operands
        arrived = leaving
        if mask > 0:
            arrived = lax.ppermute(leaving, "shard", [(s, s ^ mask * 2) for s in range(N_SHARD)])
        return (arrived, *early(slots, keys, counts, blocks))

    mask = swap_mask[0]
    arrived, sums, later = lax.switch(
        mask // 2,
        [functools.partial(branch, part) for part in range(N_SHARD // 2)],
        (leaving, swap_slots, keys, req_count, blocks),
    )
    incoming = lax.cond(
        mask % 2 == 1,
        lambda value: lax.ppermute(value, "shard", [(s, s ^ 1) for s in range(N_SHARD)]),
        lambda value: value,
        arrived,
    )
    hot_pieces = to_all_x(hot_first(swap_slots, hot_ids, blocks, incoming))
    away = to_all_x(late(0, sums, later, incoming))
    home = to_all_x(late(N_X, sums, later, incoming))
    hot_mine = hot_pick(hot_ids, hot_pieces)
    hot_block = hot_side(hot_ids, hot_mine, other_side(hot_mine))
    hot_cache = hot_last(to_all_x([hot_block] * N_X))
    crossing = other_side(away[0] + away[1] + away[2] + away[3])
    after = table_after(swap_slots, blocks, incoming)
    pooled = finish(req_count, home, crossing)
    return after.reshape(table.shape), hot_cache.reshape(1, HOT * BLOCK, E), pooled[None]


def solution(mesh):
    placed = (
        P(("shard", "rep"), None),
        P("rep"),
        P(("shard", "rep"), None),
        P("shard", None),
        P("shard", None, None),
        P("shard", None),
    )
    return jax.shard_map(
        body,
        mesh=mesh,
        in_specs=placed,
        out_specs=(P(("shard", "rep"), None), P("shard", None, None), P("shard", "rep", None)),
        check_vma=False,
    )
```

```python
import functools

import jax
import jax.numpy as jnp
from jax import lax
from jax.experimental import pallas as pl
from jax.experimental.pallas import tpu as pltpu
from jax.sharding import PartitionSpec as P

BLOCK = 128
E = 256
BLK_DEV = 16
SWAPS = 8
HOT = 4
K = 16
N_SHARD = 32
N_X = 4
N_REP = 8
OWN = 256
REQS = OWN * N_REP
PIECES = 8
HALF_ROWS = SWAPS * BLOCK
CHUNKS = 4
WIDE = E // CHUNKS
COUNT_INT = jnp.int16

SMEM = pl.BlockSpec(memory_space=pltpu.SMEM)
VMEM = pl.BlockSpec(memory_space=pltpu.VMEM)
ANY = pl.BlockSpec(memory_space=pl.ANY)


def f32(*shape):
    return jax.ShapeDtypeStruct(shape, jnp.float32)


def params(mib):
    return pltpu.CompilerParams(vmem_limit_bytes=mib * 2**20)


def cost(flops, moved):
    return pl.CostEstimate(flops=flops, bytes_accessed=moved, transcendentals=0)


def piece_owner(piece, rep):
    ahead = piece % N_X
    side = 1 - piece // N_X
    x = lax.rem(rep // 2 + ahead, N_X)
    return x * 2 + lax.rem(lax.rem(rep, 2) + side, 2)


def outgoing_kernel(slots, table, out, sems):
    copies = [
        pltpu.make_async_copy(table.at[slots[0, j]], out.at[j], sems.at[j]) for j in range(SWAPS)
    ]
    for copy in copies:
        copy.start()
    for copy in copies:
        copy.wait()


def outgoing(slots, blocks):
    return pl.pallas_call(
        outgoing_kernel,
        out_shape=f32(SWAPS, BLOCK, E),
        in_specs=[SMEM, ANY],
        out_specs=ANY,
        scratch_shapes=[pltpu.SemaphoreType.DMA((SWAPS,))],
        cost_estimate=cost(0, 2**21),
    )(slots, blocks)


def early_kernel(slots, hot, raw_keys, counts, table, sums, later, keys, flags, order, parts):
    rep = lax.axis_index("rep")

    def clear(b, carry):
        flags[b] = 0
        return carry

    def mark(j, carry):
        flags[slots[0, j]] = 1
        order[SWAPS + j] = slots[0, j]
        return carry

    def list_block(b, found):
        @pl.when(flags[b] == 0)
        def _():
            order[found] = b

        return found + 1 - flags[b]

    lax.fori_loop(0, BLK_DEV, clear, 0)
    lax.fori_loop(0, SWAPS, mark, 0)
    lax.fori_loop(0, BLK_DEV, list_block, 0)
    live = lax.broadcasted_iota(jnp.int32, (K, REQS), 0) < counts[...]
    keys[...] = jnp.where(live, raw_keys[...], -1)

    def split(j, carry):
        put_parts(table[order[j]], j, parts)
        return carry

    lax.fori_loop(0, SWAPS, split, 0)
    row_in_tile = lax.broadcasted_iota(jnp.int32, (16, 128), 0).astype(COUNT_INT)
    one, zero = jnp.bfloat16(1), jnp.bfloat16(0)

    def one_piece(piece, carry):
        start = piece_owner(piece, rep) * OWN

        def one_block(step, inner):
            j = step // 2
            side = step % 2 * 128
            lanes = pl.multiple_of(start + side, 128)
            column = pl.multiple_of(side, 128)
            place = jnp.where(j < SWAPS, PIECES, piece)
            first = (rep * BLK_DEV + order[j]) * BLOCK
            near = []
            for k in range(K):
                offset = jnp.clip(keys[pl.ds(k, 1), pl.ds(lanes, 128)] - first, -1, BLOCK)
                near.append(jnp.broadcast_to(offset, (16, 128)).astype(COUNT_INT))
            for tile in range(BLOCK // 16):
                row = row_in_tile + jnp.array(tile * 16, COUNT_INT)
                total = jnp.where(near[0] == row, one, zero)
                for k in range(1, K):
                    total = total + jnp.where(near[k] == row, one, zero)
                row0 = pl.multiple_of(j % SWAPS * BLOCK + tile * 16, 16)
                later[place, pl.ds(row0, 16), pl.ds(column, 128)] = total
            return inner

        lax.fori_loop(0, BLK_DEV * 2, one_block, 0)
        apply_counts(parts, later.at[PIECES], sums.at[piece])
        return carry

    lax.fori_loop(0, PIECES, one_piece, 0)


def turn_rows(rows):
    turned = rows.T
    high = turned.astype(jnp.bfloat16)
    return high, (turned - high.astype(jnp.float32)).astype(jnp.bfloat16)


def put_parts(rows, j, parts):
    high, low = turn_rows(rows)
    at = pl.ds(pl.multiple_of(j * BLOCK, BLOCK), BLOCK)
    for chunk in range(CHUNKS):
        parts[chunk, :WIDE, at] = high[chunk * WIDE : (chunk + 1) * WIDE]
        parts[chunk, WIDE:, at] = low[chunk * WIDE : (chunk + 1) * WIDE]


def apply_counts(parts, counted, out):
    def one_chunk(chunk, carry):
        both = jnp.dot(parts[chunk], counted[...], preferred_element_type=jnp.float32)
        out[pl.ds(pl.multiple_of(chunk * WIDE, WIDE), WIDE)] = both[:WIDE] + both[WIDE:]
        return carry

    lax.fori_loop(0, CHUNKS, one_chunk, 0)


def early(slots, hot, keys, counts, blocks):
    return pl.pallas_call(
        early_kernel,
        out_shape=(
            f32(PIECES, E, OWN),
            jax.ShapeDtypeStruct((PIECES + 1, HALF_ROWS, OWN), jnp.bfloat16),
        ),
        in_specs=[SMEM, SMEM, VMEM, VMEM, VMEM],
        out_specs=(VMEM, VMEM),
        scratch_shapes=[
            pltpu.VMEM((K, REQS), jnp.int32),
            pltpu.SMEM((BLK_DEV,), jnp.int32),
            pltpu.SMEM((BLK_DEV,), jnp.int32),
            pltpu.VMEM((CHUNKS, 2 * WIDE, HALF_ROWS), jnp.bfloat16),
        ],
        compiler_params=params(16),
        cost_estimate=cost(2**34, 2**25),
    )(slots, hot, keys, counts, blocks)


def late_kernel(sums, later, incoming, out0, out1, out2, out3, parts):
    for j in range(SWAPS):
        high, low = turn_rows(incoming[j])
        parts[:E, j * BLOCK : (j + 1) * BLOCK] = high
        parts[E:, j * BLOCK : (j + 1) * BLOCK] = low
    for ahead, out in ((2, out2), (1, out1), (3, out3), (0, out0)):
        both = jnp.dot(parts[...], later[ahead], preferred_element_type=jnp.float32)
        out[...] = sums[ahead] + both[:E] + both[E:]


def late(sums, later, incoming):
    return pl.pallas_call(
        late_kernel,
        out_shape=(f32(E, OWN),) * N_X + (jax.ShapeDtypeStruct((2 * E, HALF_ROWS), jnp.bfloat16),),
        in_specs=[VMEM] * 3,
        out_specs=(VMEM,) * (N_X + 1),
        compiler_params=params(16),
        cost_estimate=cost(2**30, 2**22),
    )(sums, later, incoming)


def home_kernel(sums, later, parts, out0, out1, out2, out3):
    for ahead, out in ((2, out2), (1, out1), (3, out3), (0, out0)):
        both = jnp.dot(parts[...], later[N_X + ahead], preferred_element_type=jnp.float32)
        out[:E] = sums[N_X + ahead] + both[:E] + both[E:]


def home(sums, later, parts):
    return pl.pallas_call(
        home_kernel,
        out_shape=(f32(E, OWN),) + (f32(E + BLOCK, OWN),) * (N_X - 1),
        in_specs=[VMEM] * 3,
        out_specs=(VMEM,) * N_X,
        compiler_params=params(16),
        cost_estimate=cost(2**30, 2**22),
    )(sums, later, parts)


def add_hot_kernel(hot, mine, other, in1, in2, in3, out1, out2, out3, hot_out, sems):
    rep = lax.axis_index("rep")
    side = lax.rem(hot[0, rep // 2] // BLK_DEV, 2)

    @pl.when(side == lax.rem(rep, 2))
    def _():
        hot_out[...] = mine[...]

    @pl.when(side != lax.rem(rep, 2))
    def _():
        hot_out[...] = other[...]

    copies = [
        pltpu.make_async_copy(hot_out, out.at[pl.ds(E, BLOCK)], sems.at[n])
        for n, out in enumerate((out1, out2, out3))
    ]
    for copy in copies:
        copy.start()
    for copy in copies:
        copy.wait()


def add_hot(hot, mine, other, homeward):
    return pl.pallas_call(
        add_hot_kernel,
        out_shape=(f32(E + BLOCK, OWN),) * (N_X - 1) + (f32(BLOCK, E),),
        in_specs=[SMEM, VMEM, VMEM, ANY, ANY, ANY],
        out_specs=(ANY, ANY, ANY, VMEM),
        input_output_aliases={3: 0, 4: 1, 5: 2},
        scratch_shapes=[pltpu.SemaphoreType.DMA((N_X - 1,))],
        compiler_params=params(8),
        cost_estimate=cost(0, 2**19),
    )(hot, mine, other, *homeward)


def hot_first_kernel(slots, hot, table, incoming, out0, out1, out2, out3):
    rep = lax.axis_index("rep")
    for ahead, out in enumerate((out0, out1, out2, out3)):
        block = lax.rem(hot[0, lax.rem(rep // 2 + ahead, N_X)], BLK_DEV)
        came = lax.fori_loop(
            0, SWAPS, lambda j, found: jnp.where(slots[0, j] == block, j, found), -1
        )

        @pl.when(came >= 0)
        def _():
            out[...] = incoming[jnp.maximum(came, 0)]

        @pl.when(came < 0)
        def _():
            out[...] = table[block]


def hot_first(slots, hot, blocks, incoming):
    return pl.pallas_call(
        hot_first_kernel,
        out_shape=(f32(BLOCK, E),) * N_X,
        in_specs=[SMEM, SMEM, VMEM, VMEM],
        out_specs=(VMEM,) * N_X,
        compiler_params=params(16),
        cost_estimate=cost(0, 2**20),
    )(slots, hot, blocks, incoming)


def hot_pick_kernel(hot, in0, in1, in2, in3, out):
    x = lax.axis_index("rep") // 2
    owner_x = hot[0, x] // (2 * BLK_DEV)
    behind = lax.rem(x - owner_x + N_X, N_X)
    for back, source in enumerate((in0, in1, in2, in3)):

        @pl.when(behind == back)
        def _():
            out[...] = source[...]


def hot_pick(hot, pieces):
    return pl.pallas_call(
        hot_pick_kernel,
        out_shape=f32(BLOCK, E),
        in_specs=[SMEM] + [VMEM] * N_X,
        out_specs=VMEM,
        compiler_params=params(8),
        cost_estimate=cost(0, 2**18),
    )(hot, *pieces)


def table_kernel(slots, table, incoming, out, came, sems):
    def clear(b, carry):
        came[b] = -1
        return carry

    def mark(j, carry):
        came[slots[0, j]] = j
        return carry

    def send(b, carry):
        @pl.when(came[b] >= 0)
        def _():
            pltpu.make_async_copy(incoming.at[jnp.maximum(came[b], 0)], out.at[b], sems.at[b]).start()

        @pl.when(came[b] < 0)
        def _():
            pltpu.make_async_copy(table.at[b], out.at[b], sems.at[b]).start()

        return carry

    def receive(b, carry):
        pltpu.make_async_copy(table.at[b], out.at[b], sems.at[b]).wait()
        return carry

    lax.fori_loop(0, BLK_DEV, clear, 0)
    lax.fori_loop(0, SWAPS, mark, 0)
    lax.fori_loop(0, BLK_DEV, send, 0)
    lax.fori_loop(0, BLK_DEV, receive, 0)


def table_after(slots, blocks, incoming):
    return pl.pallas_call(
        table_kernel,
        out_shape=f32(BLK_DEV, BLOCK, E),
        in_specs=[SMEM, VMEM, VMEM],
        out_specs=ANY,
        scratch_shapes=[pltpu.SMEM((BLK_DEV,), jnp.int32), pltpu.SemaphoreType.DMA((BLK_DEV,))],
        compiler_params=params(16),
        cost_estimate=cost(0, 2**22),
    )(slots, blocks, incoming)


def finish_kernel(counts, hot, in0, in1, in2, in3, other, pooled, hot_cache, sems):
    rep = lax.axis_index("rep")
    x = rep // 2
    blocks = (hot, in1.at[E:], in2.at[E:], in3.at[E:])
    copies = [
        pltpu.make_async_copy(block, hot_cache.at[lax.rem(x - back + N_X, N_X)], sems.at[back])
        for back, block in enumerate(blocks)
    ]
    for copy in copies:
        copy.start()
    total = in0[...] + in1[:E] + in2[:E] + in3[:E] + other[...]
    start = pl.multiple_of(rep * OWN, OWN)
    mean = total / counts[:, pl.ds(start, OWN)].astype(jnp.float32)
    pooled[...] = mean.T
    for copy in copies:
        copy.wait()


def finish(counts, hot, pieces, other):
    return pl.pallas_call(
        finish_kernel,
        out_shape=(f32(OWN, E), f32(HOT, BLOCK, E)),
        in_specs=[VMEM] * 7,
        out_specs=(VMEM, ANY),
        scratch_shapes=[pltpu.SemaphoreType.DMA((N_X,))],
        compiler_params=params(16),
        cost_estimate=cost(2**19, 2**21),
    )(counts, hot, *pieces, other)


def ahead_by(step):
    return [(x * 2 + z, (x + step) % N_X * 2 + z) for x in range(N_X) for z in range(2)]


def to_all_x(pieces):
    moved = {n: lax.ppermute(pieces[n], "rep", ahead_by(n)) for n in (2, 1, 3)}
    return [pieces[0], moved[1], moved[2], moved[3]]


def other_side(value):
    return lax.ppermute(value, "rep", [(r, r ^ 1) for r in range(N_REP)])


def body(table, swap_mask, swap_slots, hot_ids, req_idx, req_count):
    blocks = table.reshape(BLK_DEV, BLOCK, E)
    keys = req_idx[0].T
    leaving = outgoing(swap_slots, blocks)

    def branch(mask, operands):
        leaving, slots, hot, keys, counts, blocks = operands
        arrived = leaving
        if mask > 0:
            arrived = lax.ppermute(leaving, "shard", [(s, s ^ mask * 2) for s in range(N_SHARD)])
        return (arrived, *early(slots, hot, keys, counts, blocks))

    mask = swap_mask[0]
    arrived, sums, later = lax.switch(
        mask // 2,
        [functools.partial(branch, part) for part in range(N_SHARD // 2)],
        (leaving, swap_slots, hot_ids, keys, req_count, blocks),
    )
    incoming = lax.cond(
        mask % 2 == 1,
        lambda value: lax.ppermute(value, "shard", [(s, s ^ 1) for s in range(N_SHARD)]),
        lambda value: value,
        arrived,
    )
    hot_pieces = to_all_x(hot_first(swap_slots, hot_ids, blocks, incoming))
    *away, parts = late(sums, later, incoming)
    away = to_all_x(away)
    hot_mine = hot_pick(hot_ids, hot_pieces)
    own, *homeward = home(sums, later, parts)
    *homeward, hot_block = add_hot(hot_ids, hot_mine, other_side(hot_mine), homeward)
    crossing = other_side(away[0] + away[1] + away[2] + away[3])
    homeward = to_all_x([own, *homeward])
    after = table_after(swap_slots, blocks, incoming)
    pooled, hot_cache = finish(req_count, hot_block, homeward, crossing)
    return after.reshape(table.shape), hot_cache.reshape(1, HOT * BLOCK, E), pooled[None]


def solution(mesh):
    placed = (
        P(("shard", "rep"), None),
        P("rep"),
        P(("shard", "rep"), None),
        P("shard", None),
        P("shard", None, None),
        P("shard", None),
    )
    return jax.shard_map(
        body,
        mesh=mesh,
        in_specs=placed,
        out_specs=(P(("shard", "rep"), None), P("shard", None, None), P("shard", "rep", None)),
        check_vma=False,
    )
```

```python
import functools

import jax
import jax.numpy as jnp
from jax import lax
from jax.experimental import pallas as pl
from jax.experimental.pallas import tpu as pltpu
from jax.sharding import PartitionSpec as P

BLOCK = 128
E = 256
BLK_DEV = 16
SWAPS = 8
HOT = 4
K = 16
N_SHARD = 32
N_X = 4
N_REP = 8
OWN = 256
REQS = OWN * N_REP
PIECES = 8
HALF_ROWS = SWAPS * BLOCK
CHUNKS = 4
WIDE = E // CHUNKS
COUNT_INT = jnp.int16

SMEM = pl.BlockSpec(memory_space=pltpu.SMEM)
VMEM = pl.BlockSpec(memory_space=pltpu.VMEM)
ANY = pl.BlockSpec(memory_space=pl.ANY)


def in_vmem(value):
    return pltpu.with_memory_space_constraint(value, pltpu.VMEM)


def f32(*shape):
    return jax.ShapeDtypeStruct(shape, jnp.float32)


def params(mib):
    return pltpu.CompilerParams(vmem_limit_bytes=mib * 2**20)


def cost(flops, moved):
    return pl.CostEstimate(flops=flops, bytes_accessed=moved, transcendentals=0)


def piece_owner(piece, rep):
    ahead = piece % N_X
    side = 1 - piece // N_X
    x = lax.rem(rep // 2 + ahead, N_X)
    return x * 2 + lax.rem(lax.rem(rep, 2) + side, 2)


def outgoing_kernel(slots, table, out, sems):
    copies = [
        pltpu.make_async_copy(table.at[slots[0, j]], out.at[j], sems.at[j]) for j in range(SWAPS)
    ]
    for copy in copies:
        copy.start()
    for copy in copies:
        copy.wait()


def outgoing(slots, blocks):
    return pl.pallas_call(
        outgoing_kernel,
        out_shape=f32(SWAPS, BLOCK, E),
        in_specs=[SMEM, ANY],
        out_specs=ANY,
        scratch_shapes=[pltpu.SemaphoreType.DMA((SWAPS,))],
        cost_estimate=cost(0, 2**21),
    )(slots, blocks)


def early_kernel(slots, hot, raw_keys, counts, table, sums, later_away, later_home, hot_kept, keys, flags, order, parts, now):
    rep = lax.axis_index("rep")

    def clear(b, carry):
        flags[b] = 0
        return carry

    def mark(j, carry):
        flags[slots[0, j]] = 1
        order[SWAPS + j] = slots[0, j]
        return carry

    def list_block(b, found):
        @pl.when(flags[b] == 0)
        def _():
            order[found] = b

        return found + 1 - flags[b]

    lax.fori_loop(0, BLK_DEV, clear, 0)
    lax.fori_loop(0, SWAPS, mark, 0)
    lax.fori_loop(0, BLK_DEV, list_block, 0)
    live = lax.broadcasted_iota(jnp.int32, (K, REQS), 0) < counts[...]
    keys[...] = jnp.where(live, raw_keys[...], -1)

    def split(j, carry):
        put_parts(table[order[j]], j, parts)
        return carry

    lax.fori_loop(0, SWAPS, split, 0)
    def keep_hot(n, carry):
        hot_kept[n] = table[lax.rem(hot[0, lax.rem(rep // 2 + n + 1, N_X)], BLK_DEV)]
        return carry

    lax.fori_loop(0, N_X - 1, keep_hot, 0)
    row_in_tile = lax.broadcasted_iota(jnp.int32, (16, 128), 0).astype(COUNT_INT)
    one, zero = jnp.bfloat16(1), jnp.bfloat16(0)

    def one_piece(piece, carry):
        start = piece_owner(piece, rep) * OWN

        def one_block(step, inner):
            j = step // 2
            side = step % 2 * 128
            lanes = pl.multiple_of(start + side, 128)
            column = pl.multiple_of(side, 128)
            first = (rep * BLK_DEV + order[j]) * BLOCK
            near = []
            for k in range(K):
                offset = jnp.clip(keys[pl.ds(k, 1), pl.ds(lanes, 128)] - first, -1, BLOCK)
                near.append(jnp.broadcast_to(offset, (16, 128)).astype(COUNT_INT))
            tiles = []
            for tile in range(BLOCK // 16):
                row = row_in_tile + jnp.array(tile * 16, COUNT_INT)
                total = jnp.where(near[0] == row, one, zero)
                for k in range(1, K):
                    total = total + jnp.where(near[k] == row, one, zero)
                tiles.append(total)
            row0 = pl.multiple_of(j % SWAPS * BLOCK, BLOCK)

            def keep(place):
                for tile, total in enumerate(tiles):
                    place[pl.ds(row0 + tile * 16, 16), pl.ds(column, 128)] = total

            @pl.when(j < SWAPS)
            def _():
                keep(now)

            @pl.when(jnp.logical_and(j >= SWAPS, piece < N_X))
            def _():
                keep(later_away.at[jnp.minimum(piece, N_X - 1)])

            @pl.when(jnp.logical_and(j >= SWAPS, piece >= N_X))
            def _():
                keep(later_home.at[jnp.maximum(piece - N_X, 0)])

            return inner

        lax.fori_loop(0, BLK_DEV * 2, one_block, 0)
        apply_counts(parts, now, sums.at[piece])
        return carry

    lax.fori_loop(0, PIECES, one_piece, 0)


def turn_rows(rows):
    turned = rows.T
    high = turned.astype(jnp.bfloat16)
    return high, (turned - high.astype(jnp.float32)).astype(jnp.bfloat16)


def put_parts(rows, j, parts):
    high, low = turn_rows(rows)
    at = pl.ds(pl.multiple_of(j * BLOCK, BLOCK), BLOCK)
    for chunk in range(CHUNKS):
        parts[chunk, :WIDE, at] = high[chunk * WIDE : (chunk + 1) * WIDE]
        parts[chunk, WIDE:, at] = low[chunk * WIDE : (chunk + 1) * WIDE]


def apply_counts(parts, counted, out):
    def one_chunk(chunk, carry):
        both = jnp.dot(parts[chunk], counted[...], preferred_element_type=jnp.float32)
        out[pl.ds(pl.multiple_of(chunk * WIDE, WIDE), WIDE)] = both[:WIDE] + both[WIDE:]
        return carry

    lax.fori_loop(0, CHUNKS, one_chunk, 0)


def early(slots, hot, keys, counts, blocks):
    return pl.pallas_call(
        early_kernel,
        out_shape=(
            f32(PIECES, E, OWN),
            jax.ShapeDtypeStruct((N_X, HALF_ROWS, OWN), jnp.bfloat16),
            jax.ShapeDtypeStruct((N_X, HALF_ROWS, OWN), jnp.bfloat16),
            f32(N_X - 1, BLOCK, E),
        ),
        in_specs=[SMEM, SMEM, VMEM, VMEM, VMEM],
        out_specs=(VMEM,) * 4,
        scratch_shapes=[
            pltpu.VMEM((K, REQS), jnp.int32),
            pltpu.SMEM((BLK_DEV,), jnp.int32),
            pltpu.SMEM((BLK_DEV,), jnp.int32),
            pltpu.VMEM((CHUNKS, 2 * WIDE, HALF_ROWS), jnp.bfloat16),
            pltpu.VMEM((HALF_ROWS, OWN), jnp.bfloat16),
        ],
        compiler_params=params(16),
        cost_estimate=cost(2**34, 2**25),
    )(slots, hot, keys, counts, blocks)


def late_kernel(sums, later, incoming, out0, out1, out2, out3, parts, sums_in, sem):
    copy = pltpu.make_async_copy(sums.at[pl.ds(0, N_X)], sums_in, sem.at[0])
    copy.start()
    for j in range(SWAPS):
        high, low = turn_rows(incoming[j])
        parts[:E, j * BLOCK : (j + 1) * BLOCK] = high
        parts[E:, j * BLOCK : (j + 1) * BLOCK] = low
    copy.wait()
    for ahead, out in ((2, out2), (1, out1), (3, out3), (0, out0)):
        both = jnp.dot(parts[...], later[ahead], preferred_element_type=jnp.float32)
        out[...] = sums_in[ahead] + both[:E] + both[E:]


def late(sums, later, incoming):
    return pl.pallas_call(
        late_kernel,
        out_shape=(f32(E, OWN),) * N_X + (jax.ShapeDtypeStruct((2 * E, HALF_ROWS), jnp.bfloat16),),
        in_specs=[ANY, VMEM, VMEM],
        out_specs=(VMEM,) * (N_X + 1),
        scratch_shapes=[pltpu.VMEM((N_X, E, OWN), jnp.float32), pltpu.SemaphoreType.DMA((1,))],
        compiler_params=params(16),
        cost_estimate=cost(2**30, 2**22),
    )(sums, in_vmem(later), in_vmem(incoming))


def home_kernel(sums, later, parts, out0, out1, out2, out3, sums_in, sem):
    copy = pltpu.make_async_copy(sums.at[pl.ds(N_X, N_X)], sums_in, sem.at[0])
    copy.start()
    copy.wait()
    for ahead, out in ((2, out2), (1, out1), (3, out3), (0, out0)):
        both = jnp.dot(parts[...], later[ahead], preferred_element_type=jnp.float32)
        out[:E] = sums_in[ahead] + both[:E] + both[E:]


def home(sums, later, parts):
    return pl.pallas_call(
        home_kernel,
        out_shape=(f32(E, OWN),) + (f32(E + BLOCK, OWN),) * (N_X - 1),
        in_specs=[ANY, VMEM, VMEM],
        out_specs=(VMEM,) * N_X,
        scratch_shapes=[pltpu.VMEM((N_X, E, OWN), jnp.float32), pltpu.SemaphoreType.DMA((1,))],
        compiler_params=params(16),
        cost_estimate=cost(2**30, 2**22),
    )(sums, later, parts)


def add_hot_kernel(hot, mine, other, in1, in2, in3, out1, out2, out3, hot_out, sems):
    rep = lax.axis_index("rep")
    side = lax.rem(hot[0, rep // 2] // BLK_DEV, 2)

    @pl.when(side == lax.rem(rep, 2))
    def _():
        hot_out[...] = mine[...]

    @pl.when(side != lax.rem(rep, 2))
    def _():
        hot_out[...] = other[...]

    copies = [
        pltpu.make_async_copy(hot_out, out.at[pl.ds(E, BLOCK)], sems.at[n])
        for n, out in enumerate((out1, out2, out3))
    ]
    for copy in copies:
        copy.start()
    for copy in copies:
        copy.wait()


def add_hot(hot, mine, other, homeward):
    return pl.pallas_call(
        add_hot_kernel,
        out_shape=(f32(E + BLOCK, OWN),) * (N_X - 1) + (f32(BLOCK, E),),
        in_specs=[SMEM, VMEM, VMEM, ANY, ANY, ANY],
        out_specs=(ANY, ANY, ANY, VMEM),
        input_output_aliases={3: 0, 4: 1, 5: 2},
        scratch_shapes=[pltpu.SemaphoreType.DMA((N_X - 1,))],
        compiler_params=params(8),
        cost_estimate=cost(0, 2**19),
    )(hot, mine, other, *homeward)


def came_from(slots, block):
    return lax.fori_loop(
        0, SWAPS, lambda j, found: jnp.where(slots[0, j] == block, j, found), -1
    )


def hot_first_kernel(slots, hot, kept, incoming, out1, out2, out3):
    x = lax.axis_index("rep") // 2
    for n, out in enumerate((out1, out2, out3)):
        block = lax.rem(hot[0, lax.rem(x + n + 1, N_X)], BLK_DEV)
        came = came_from(slots, block)

        @pl.when(came >= 0)
        def _():
            out[...] = incoming[jnp.maximum(came, 0)]

        @pl.when(came < 0)
        def _():
            out[...] = kept[n]


def hot_first(slots, hot, kept, incoming):
    return pl.pallas_call(
        hot_first_kernel,
        out_shape=(f32(BLOCK, E),) * (N_X - 1),
        in_specs=[SMEM, SMEM, VMEM, VMEM],
        out_specs=(VMEM,) * (N_X - 1),
        compiler_params=params(8),
        cost_estimate=cost(0, 2**20),
    )(slots, hot, in_vmem(kept), in_vmem(incoming))


def hot_pick_kernel(slots, hot, table, incoming, in1, in2, in3, out, sem):
    x = lax.axis_index("rep") // 2
    owner_x = hot[0, x] // (2 * BLK_DEV)
    behind = lax.rem(x - owner_x + N_X, N_X)
    block = lax.rem(hot[0, x], BLK_DEV)
    came = came_from(slots, block)
    for n, source in enumerate((in1, in2, in3)):

        @pl.when(behind == n + 1)
        def _():
            out[...] = source[...]

    @pl.when(jnp.logical_and(behind == 0, came >= 0))
    def _():
        out[...] = incoming[jnp.maximum(came, 0)]

    @pl.when(jnp.logical_and(behind == 0, came < 0))
    def _():
        copy = pltpu.make_async_copy(table.at[block], out, sem.at[0])
        copy.start()
        copy.wait()


def hot_pick(slots, hot, blocks, incoming, pieces):
    return pl.pallas_call(
        hot_pick_kernel,
        out_shape=f32(BLOCK, E),
        in_specs=[SMEM, SMEM, ANY, VMEM] + [VMEM] * (N_X - 1),
        out_specs=VMEM,
        scratch_shapes=[pltpu.SemaphoreType.DMA((1,))],
        compiler_params=params(8),
        cost_estimate=cost(0, 2**18),
    )(slots, hot, blocks, in_vmem(incoming), *pieces)


def table_kernel(slots, table, incoming, out, came, sems):
    def clear(b, carry):
        came[b] = -1
        return carry

    def mark(j, carry):
        came[slots[0, j]] = j
        return carry

    def send(b, carry):
        @pl.when(came[b] >= 0)
        def _():
            pltpu.make_async_copy(incoming.at[jnp.maximum(came[b], 0)], out.at[b], sems.at[b]).start()

        @pl.when(came[b] < 0)
        def _():
            pltpu.make_async_copy(table.at[b], out.at[b], sems.at[b]).start()

        return carry

    def receive(b, carry):
        pltpu.make_async_copy(table.at[b], out.at[b], sems.at[b]).wait()
        return carry

    lax.fori_loop(0, BLK_DEV, clear, 0)
    lax.fori_loop(0, SWAPS, mark, 0)
    lax.fori_loop(0, BLK_DEV, send, 0)
    lax.fori_loop(0, BLK_DEV, receive, 0)


def table_after(slots, blocks, incoming):
    return pl.pallas_call(
        table_kernel,
        out_shape=f32(BLK_DEV, BLOCK, E),
        in_specs=[SMEM, VMEM, VMEM],
        out_specs=ANY,
        scratch_shapes=[pltpu.SMEM((BLK_DEV,), jnp.int32), pltpu.SemaphoreType.DMA((BLK_DEV,))],
        compiler_params=params(16),
        cost_estimate=cost(0, 2**22),
    )(slots, blocks, incoming)


def finish_kernel(counts, hot, in0, in1, in2, in3, other, pooled, hot_cache, sems):
    rep = lax.axis_index("rep")
    x = rep // 2
    blocks = (hot, in1.at[E:], in2.at[E:], in3.at[E:])
    copies = [
        pltpu.make_async_copy(block, hot_cache.at[lax.rem(x - back + N_X, N_X)], sems.at[back])
        for back, block in enumerate(blocks)
    ]
    for copy in copies:
        copy.start()
    total = in0[...] + in1[:E] + in2[:E] + in3[:E] + other[...]
    start = pl.multiple_of(rep * OWN, OWN)
    mean = total / counts[:, pl.ds(start, OWN)].astype(jnp.float32)
    pooled[...] = mean.T
    for copy in copies:
        copy.wait()


def finish(counts, hot, pieces, other):
    return pl.pallas_call(
        finish_kernel,
        out_shape=(f32(OWN, E), f32(HOT, BLOCK, E)),
        in_specs=[VMEM] * 7,
        out_specs=(VMEM, ANY),
        scratch_shapes=[pltpu.SemaphoreType.DMA((N_X,))],
        compiler_params=params(16),
        cost_estimate=cost(2**19, 2**21),
    )(counts, hot, *pieces, other)


def ahead_by(step):
    return [(x * 2 + z, (x + step) % N_X * 2 + z) for x in range(N_X) for z in range(2)]


def to_all_x(pieces):
    moved = {n: lax.ppermute(pieces[n], "rep", ahead_by(n)) for n in (2, 1, 3)}
    return [pieces[0], moved[1], moved[2], moved[3]]


def other_side(value):
    return lax.ppermute(value, "rep", [(r, r ^ 1) for r in range(N_REP)])


def body(table, swap_mask, swap_slots, hot_ids, req_idx, req_count):
    blocks = table.reshape(BLK_DEV, BLOCK, E)
    keys = req_idx[0].T
    leaving = outgoing(swap_slots, blocks)

    def branch(mask, operands):
        leaving, slots, hot, keys, counts, blocks = operands
        arrived = leaving
        if mask > 0:
            arrived = lax.ppermute(leaving, "shard", [(s, s ^ mask * 2) for s in range(N_SHARD)])
        return (arrived, *early(slots, hot, keys, counts, blocks))

    mask = swap_mask[0]
    arrived, sums, later_away, later_home, hot_kept = lax.switch(
        mask // 2,
        [functools.partial(branch, part) for part in range(N_SHARD // 2)],
        (leaving, swap_slots, hot_ids, keys, req_count, blocks),
    )
    incoming = lax.cond(
        mask % 2 == 1,
        lambda value: lax.ppermute(value, "shard", [(s, s ^ 1) for s in range(N_SHARD)]),
        lambda value: value,
        arrived,
    )
    hot_pieces = to_all_x([None, *hot_first(swap_slots, hot_ids, hot_kept, incoming)])[1:]
    *away, parts = late(sums, later_away, incoming)
    away = to_all_x(away)
    hot_mine = hot_pick(swap_slots, hot_ids, blocks, incoming, hot_pieces)
    own, *homeward = home(sums, later_home, parts)
    *homeward, hot_block = add_hot(hot_ids, hot_mine, other_side(hot_mine), homeward)
    crossing = other_side(away[0] + away[1] + away[2] + away[3])
    homeward = to_all_x([own, *homeward])
    after = table_after(swap_slots, blocks, incoming)
    pooled, hot_cache = finish(req_count, hot_block, homeward, crossing)
    return after.reshape(table.shape), hot_cache.reshape(1, HOT * BLOCK, E), pooled[None]


def solution(mesh):
    placed = (
        P(("shard", "rep"), None),
        P("rep"),
        P(("shard", "rep"), None),
        P("shard", None),
        P("shard", None, None),
        P("shard", None),
    )
    return jax.shard_map(
        body,
        mesh=mesh,
        in_specs=placed,
        out_specs=(P(("shard", "rep"), None), P("shard", None, None), P("shard", "rep", None)),
        check_vma=False,
    )
```

```python
import functools

import jax
import jax.numpy as jnp
from jax import lax
from jax.experimental import pallas as pl
from jax.experimental.pallas import tpu as pltpu
from jax.sharding import PartitionSpec as P

BLOCK = 128
E = 256
BLK_DEV = 16
SWAPS = 8
HOT = 4
K = 16
N_SHARD = 32
N_X = 4
N_REP = 8
OWN = 256
REQS = OWN * N_REP
PIECES = 8
HALF_ROWS = SWAPS * BLOCK
CHUNKS = 4
WIDE = E // CHUNKS
COUNT_INT = jnp.int16

SMEM = pl.BlockSpec(memory_space=pltpu.SMEM)
VMEM = pl.BlockSpec(memory_space=pltpu.VMEM)
ANY = pl.BlockSpec(memory_space=pl.ANY)


def in_vmem(value):
    return pltpu.with_memory_space_constraint(value, pltpu.VMEM)


def f32(*shape):
    return jax.ShapeDtypeStruct(shape, jnp.float32)


def params(mib):
    return pltpu.CompilerParams(vmem_limit_bytes=mib * 2**20)


def cost(flops, moved):
    return pl.CostEstimate(flops=flops, bytes_accessed=moved, transcendentals=0)


def piece_owner(piece, rep):
    ahead = piece % N_X
    side = 1 - piece // N_X
    x = lax.rem(rep // 2 + ahead, N_X)
    return x * 2 + lax.rem(lax.rem(rep, 2) + side, 2)


def outgoing_kernel(slots, table, out, sems):
    copies = [
        pltpu.make_async_copy(table.at[slots[0, j]], out.at[j], sems.at[j]) for j in range(SWAPS)
    ]
    for copy in copies:
        copy.start()
    for copy in copies:
        copy.wait()


def outgoing(slots, blocks):
    return pl.pallas_call(
        outgoing_kernel,
        out_shape=f32(SWAPS, BLOCK, E),
        in_specs=[SMEM, ANY],
        out_specs=ANY,
        scratch_shapes=[pltpu.SemaphoreType.DMA((SWAPS,))],
        cost_estimate=cost(0, 2**21),
    )(slots, blocks)


def early_kernel(slots, hot, raw_keys, counts, table, sums, later_away, later_home, hot_kept, keys, flags, order, parts, now):
    rep = lax.axis_index("rep")

    def clear(b, carry):
        flags[b] = 0
        return carry

    def mark(j, carry):
        flags[slots[0, j]] = 1
        order[SWAPS + j] = slots[0, j]
        return carry

    def list_block(b, found):
        @pl.when(flags[b] == 0)
        def _():
            order[found] = b

        return found + 1 - flags[b]

    lax.fori_loop(0, BLK_DEV, clear, 0)
    lax.fori_loop(0, SWAPS, mark, 0)
    lax.fori_loop(0, BLK_DEV, list_block, 0)
    live = lax.broadcasted_iota(jnp.int32, (K, REQS), 0) < counts[...]
    keys[...] = jnp.where(live, raw_keys[...], -1)

    def split(j, carry):
        put_parts(table[order[j]], j, parts)
        return carry

    lax.fori_loop(0, SWAPS, split, 0)
    def keep_hot(n, carry):
        hot_kept[n] = table[lax.rem(hot[0, lax.rem(rep // 2 + n + 1, N_X)], BLK_DEV)]
        return carry

    lax.fori_loop(0, N_X - 1, keep_hot, 0)
    row_in_tile = lax.broadcasted_iota(jnp.int32, (16, 128), 0).astype(COUNT_INT)
    one, zero = jnp.bfloat16(1), jnp.bfloat16(0)

    def one_piece(piece, carry):
        start = piece_owner(piece, rep) * OWN

        def one_block(step, inner):
            j = step // 2
            side = step % 2 * 128
            lanes = pl.multiple_of(start + side, 128)
            column = pl.multiple_of(side, 128)
            first = (rep * BLK_DEV + order[j]) * BLOCK
            near = []
            for k in range(K):
                offset = jnp.clip(keys[pl.ds(k, 1), pl.ds(lanes, 128)] - first, -1, BLOCK)
                near.append(jnp.broadcast_to(offset, (16, 128)).astype(COUNT_INT))
            tiles = []
            for tile in range(BLOCK // 16):
                row = row_in_tile + jnp.array(tile * 16, COUNT_INT)
                total = jnp.where(near[0] == row, one, zero)
                for k in range(1, K):
                    total = total + jnp.where(near[k] == row, one, zero)
                tiles.append(total)
            row0 = pl.multiple_of(j % SWAPS * BLOCK, BLOCK)

            def keep(place):
                for tile, total in enumerate(tiles):
                    place[pl.ds(row0 + tile * 16, 16), pl.ds(column, 128)] = total

            @pl.when(j < SWAPS)
            def _():
                keep(now)

            @pl.when(jnp.logical_and(j >= SWAPS, piece < N_X))
            def _():
                keep(later_away.at[jnp.minimum(piece, N_X - 1)])

            @pl.when(jnp.logical_and(j >= SWAPS, piece >= N_X))
            def _():
                keep(later_home.at[jnp.maximum(piece - N_X, 0)])

            return inner

        lax.fori_loop(0, BLK_DEV * 2, one_block, 0)
        apply_counts(parts, now, sums.at[piece])
        return carry

    lax.fori_loop(0, PIECES, one_piece, 0)


def turn_rows(rows):
    turned = rows.T
    high = turned.astype(jnp.bfloat16)
    return high, (turned - high.astype(jnp.float32)).astype(jnp.bfloat16)


def put_parts(rows, j, parts):
    high, low = turn_rows(rows)
    at = pl.ds(pl.multiple_of(j * BLOCK, BLOCK), BLOCK)
    for chunk in range(CHUNKS):
        parts[chunk, :WIDE, at] = high[chunk * WIDE : (chunk + 1) * WIDE]
        parts[chunk, WIDE:, at] = low[chunk * WIDE : (chunk + 1) * WIDE]


def apply_counts(parts, counted, out):
    def one_chunk(chunk, carry):
        both = jnp.dot(parts[chunk], counted[...], preferred_element_type=jnp.float32)
        out[pl.ds(pl.multiple_of(chunk * WIDE, WIDE), WIDE)] = both[:WIDE] + both[WIDE:]
        return carry

    lax.fori_loop(0, CHUNKS, one_chunk, 0)


def early(slots, hot, keys, counts, blocks):
    return pl.pallas_call(
        early_kernel,
        out_shape=(
            f32(PIECES, E, OWN),
            jax.ShapeDtypeStruct((N_X, HALF_ROWS, OWN), jnp.bfloat16),
            jax.ShapeDtypeStruct((N_X, HALF_ROWS, OWN), jnp.bfloat16),
            f32(N_X - 1, BLOCK, E),
        ),
        in_specs=[SMEM, SMEM, VMEM, VMEM, VMEM],
        out_specs=(VMEM,) * 4,
        scratch_shapes=[
            pltpu.VMEM((K, REQS), jnp.int32),
            pltpu.SMEM((BLK_DEV,), jnp.int32),
            pltpu.SMEM((BLK_DEV,), jnp.int32),
            pltpu.VMEM((CHUNKS, 2 * WIDE, HALF_ROWS), jnp.bfloat16),
            pltpu.VMEM((HALF_ROWS, OWN), jnp.bfloat16),
        ],
        compiler_params=params(16),
        cost_estimate=cost(2**34, 2**25),
    )(slots, hot, keys, counts, blocks)


def late_kernel(sums, later, incoming, out0, out1, out2, out3, parts, sums_in, sem):
    copy = pltpu.make_async_copy(sums.at[pl.ds(0, N_X)], sums_in, sem.at[0])
    copy.start()
    for j in range(SWAPS):
        high, low = turn_rows(incoming[j])
        parts[:E, j * BLOCK : (j + 1) * BLOCK] = high
        parts[E:, j * BLOCK : (j + 1) * BLOCK] = low
    copy.wait()
    for ahead, out in ((2, out2), (1, out1), (3, out3), (0, out0)):
        both = jnp.dot(parts[...], later[ahead], preferred_element_type=jnp.float32)
        out[...] = sums_in[ahead] + both[:E] + both[E:]


def late(sums, later, incoming):
    return pl.pallas_call(
        late_kernel,
        out_shape=(f32(E, OWN),) * N_X + (jax.ShapeDtypeStruct((2 * E, HALF_ROWS), jnp.bfloat16),),
        in_specs=[ANY, VMEM, VMEM],
        out_specs=(VMEM,) * (N_X + 1),
        scratch_shapes=[pltpu.VMEM((N_X, E, OWN), jnp.float32), pltpu.SemaphoreType.DMA((1,))],
        compiler_params=params(16),
        cost_estimate=cost(2**30, 2**22),
    )(sums, in_vmem(later), in_vmem(incoming))


def home_kernel(sums, later, parts, out0, out1, out2, out3, sums_in, sem):
    copy = pltpu.make_async_copy(sums.at[pl.ds(N_X, N_X)], sums_in, sem.at[0])
    copy.start()
    copy.wait()
    for ahead, out in ((2, out2), (1, out1), (3, out3), (0, out0)):
        both = jnp.dot(parts[...], later[ahead], preferred_element_type=jnp.float32)
        out[:E] = sums_in[ahead] + both[:E] + both[E:]


def home(sums, later, parts):
    return pl.pallas_call(
        home_kernel,
        out_shape=(f32(E, OWN),) + (f32(E + BLOCK, OWN),) * (N_X - 1),
        in_specs=[ANY, VMEM, VMEM],
        out_specs=(VMEM,) * N_X,
        scratch_shapes=[pltpu.VMEM((N_X, E, OWN), jnp.float32), pltpu.SemaphoreType.DMA((1,))],
        compiler_params=params(16),
        cost_estimate=cost(2**30, 2**22),
    )(sums, later, parts)


def add_hot_kernel(hot, mine, other, in1, in2, in3, out1, out2, out3, hot_out, sems):
    rep = lax.axis_index("rep")
    side = lax.rem(hot[0, rep // 2] // BLK_DEV, 2)

    @pl.when(side == lax.rem(rep, 2))
    def _():
        hot_out[...] = mine[...]

    @pl.when(side != lax.rem(rep, 2))
    def _():
        hot_out[...] = other[...]

    copies = [
        pltpu.make_async_copy(hot_out, out.at[pl.ds(E, BLOCK)], sems.at[n])
        for n, out in enumerate((out1, out2, out3))
    ]
    for copy in copies:
        copy.start()
    for copy in copies:
        copy.wait()


def add_hot(hot, mine, other, homeward):
    return pl.pallas_call(
        add_hot_kernel,
        out_shape=(f32(E + BLOCK, OWN),) * (N_X - 1) + (f32(BLOCK, E),),
        in_specs=[SMEM, VMEM, VMEM, ANY, ANY, ANY],
        out_specs=(ANY, ANY, ANY, VMEM),
        input_output_aliases={3: 0, 4: 1, 5: 2},
        scratch_shapes=[pltpu.SemaphoreType.DMA((N_X - 1,))],
        compiler_params=params(8),
        cost_estimate=cost(0, 2**19),
    )(hot, mine, other, *homeward)


def came_from(slots, block):
    return lax.fori_loop(
        0, SWAPS, lambda j, found: jnp.where(slots[0, j] == block, j, found), -1
    )


def hot_first_kernel(slots, hot, kept, incoming, out1, out2, out3):
    x = lax.axis_index("rep") // 2
    for n, out in enumerate((out1, out2, out3)):
        block = lax.rem(hot[0, lax.rem(x + n + 1, N_X)], BLK_DEV)
        came = came_from(slots, block)

        @pl.when(came >= 0)
        def _():
            out[...] = incoming[jnp.maximum(came, 0)]

        @pl.when(came < 0)
        def _():
            out[...] = kept[n]


def hot_first(slots, hot, kept, incoming):
    return pl.pallas_call(
        hot_first_kernel,
        out_shape=(f32(BLOCK, E),) * (N_X - 1),
        in_specs=[SMEM, SMEM, VMEM, VMEM],
        out_specs=(VMEM,) * (N_X - 1),
        compiler_params=params(8),
        cost_estimate=cost(0, 2**20),
    )(slots, hot, in_vmem(kept), in_vmem(incoming))


def hot_pick_kernel(slots, hot, table, incoming, in1, in3, in2, out, sem):
    x = lax.axis_index("rep") // 2
    owner_x = hot[0, x] // (2 * BLK_DEV)
    behind = lax.rem(x - owner_x + N_X, N_X)
    block = lax.rem(hot[0, x], BLK_DEV)
    came = came_from(slots, block)
    for n, source in enumerate((in1, in2, in3)):

        @pl.when(behind == n + 1)
        def _():
            out[...] = source[...]

    @pl.when(jnp.logical_and(behind == 0, came >= 0))
    def _():
        out[...] = incoming[jnp.maximum(came, 0)]

    @pl.when(jnp.logical_and(behind == 0, came < 0))
    def _():
        copy = pltpu.make_async_copy(table.at[block], out, sem.at[0])
        copy.start()
        copy.wait()


def hot_pick(slots, hot, blocks, incoming, pieces):
    return pl.pallas_call(
        hot_pick_kernel,
        out_shape=f32(BLOCK, E),
        in_specs=[SMEM, SMEM, ANY, VMEM] + [VMEM] * (N_X - 1),
        out_specs=VMEM,
        scratch_shapes=[pltpu.SemaphoreType.DMA((1,))],
        compiler_params=params(8),
        cost_estimate=cost(0, 2**18),
    )(slots, hot, blocks, in_vmem(incoming), *[pieces[n] for n in (0, 2, 1)])


def table_kernel(slots, table, incoming, out, came, sems):
    def clear(b, carry):
        came[b] = -1
        return carry

    def mark(j, carry):
        came[slots[0, j]] = j
        return carry

    def send(b, carry):
        @pl.when(came[b] >= 0)
        def _():
            pltpu.make_async_copy(incoming.at[jnp.maximum(came[b], 0)], out.at[b], sems.at[b]).start()

        @pl.when(came[b] < 0)
        def _():
            pltpu.make_async_copy(table.at[b], out.at[b], sems.at[b]).start()

        return carry

    def receive(b, carry):
        pltpu.make_async_copy(table.at[b], out.at[b], sems.at[b]).wait()
        return carry

    lax.fori_loop(0, BLK_DEV, clear, 0)
    lax.fori_loop(0, SWAPS, mark, 0)
    lax.fori_loop(0, BLK_DEV, send, 0)
    lax.fori_loop(0, BLK_DEV, receive, 0)


def table_after(slots, blocks, incoming):
    return pl.pallas_call(
        table_kernel,
        out_shape=f32(BLK_DEV, BLOCK, E),
        in_specs=[SMEM, VMEM, VMEM],
        out_specs=ANY,
        scratch_shapes=[pltpu.SMEM((BLK_DEV,), jnp.int32), pltpu.SemaphoreType.DMA((BLK_DEV,))],
        compiler_params=params(16),
        cost_estimate=cost(0, 2**22),
    )(slots, blocks, incoming)


def finish_kernel(counts, hot, in0, in1, in3, in2, other, pooled, hot_cache, sems):
    rep = lax.axis_index("rep")
    x = rep // 2
    blocks = (hot, in1.at[E:], in2.at[E:], in3.at[E:])
    copies = [
        pltpu.make_async_copy(block, hot_cache.at[lax.rem(x - back + N_X, N_X)], sems.at[back])
        for back, block in enumerate(blocks)
    ]
    for copy in copies:
        copy.start()
    total = in0[...] + in1[:E] + in2[:E] + in3[:E] + other[...]
    start = pl.multiple_of(rep * OWN, OWN)
    mean = total / counts[:, pl.ds(start, OWN)].astype(jnp.float32)
    pooled[...] = mean.T
    for copy in copies:
        copy.wait()


def finish(counts, hot, pieces, other):
    return pl.pallas_call(
        finish_kernel,
        out_shape=(f32(OWN, E), f32(HOT, BLOCK, E)),
        in_specs=[VMEM] * 7,
        out_specs=(VMEM, ANY),
        scratch_shapes=[pltpu.SemaphoreType.DMA((N_X,))],
        compiler_params=params(16),
        cost_estimate=cost(2**19, 2**21),
    )(counts, hot, *[pieces[n] for n in (0, 1, 3, 2)], other)


def ahead_by(step):
    return [(x * 2 + z, (x + step) % N_X * 2 + z) for x in range(N_X) for z in range(2)]


def to_all_x(pieces):
    moved = {n: lax.ppermute(pieces[n], "rep", ahead_by(n)) for n in (2, 1, 3)}
    return [pieces[0], moved[1], moved[2], moved[3]]


def other_side(value):
    return lax.ppermute(value, "rep", [(r, r ^ 1) for r in range(N_REP)])


def body(table, swap_mask, swap_slots, hot_ids, req_idx, req_count):
    blocks = table.reshape(BLK_DEV, BLOCK, E)
    keys = req_idx[0].T
    leaving = outgoing(swap_slots, blocks)

    def branch(mask, operands):
        leaving, slots, hot, keys, counts, blocks = operands
        arrived = leaving
        if mask > 0:
            arrived = lax.ppermute(leaving, "shard", [(s, s ^ mask * 2) for s in range(N_SHARD)])
        return (arrived, *early(slots, hot, keys, counts, blocks))

    mask = swap_mask[0]
    arrived, sums, later_away, later_home, hot_kept = lax.switch(
        mask // 2,
        [functools.partial(branch, part) for part in range(N_SHARD // 2)],
        (leaving, swap_slots, hot_ids, keys, req_count, blocks),
    )
    incoming = lax.cond(
        mask % 2 == 1,
        lambda value: lax.ppermute(value, "shard", [(s, s ^ 1) for s in range(N_SHARD)]),
        lambda value: value,
        arrived,
    )
    hot_pieces = to_all_x([None, *hot_first(swap_slots, hot_ids, hot_kept, incoming)])[1:]
    *away, parts = late(sums, later_away, incoming)
    away = to_all_x(away)
    hot_mine = hot_pick(swap_slots, hot_ids, blocks, incoming, hot_pieces)
    own, *homeward = home(sums, later_home, parts)
    *homeward, hot_block = add_hot(hot_ids, hot_mine, other_side(hot_mine), homeward)
    crossing = other_side(away[0] + away[1] + away[3] + away[2])
    homeward = to_all_x([own, *homeward])
    after = table_after(swap_slots, blocks, incoming)
    pooled, hot_cache = finish(req_count, hot_block, homeward, crossing)
    return after.reshape(table.shape), hot_cache.reshape(1, HOT * BLOCK, E), pooled[None]


def solution(mesh):
    placed = (
        P(("shard", "rep"), None),
        P("rep"),
        P(("shard", "rep"), None),
        P("shard", None),
        P("shard", None, None),
        P("shard", None),
    )
    return jax.shard_map(
        body,
        mesh=mesh,
        in_specs=placed,
        out_specs=(P(("shard", "rep"), None), P("shard", None, None), P("shard", "rep", None)),
        check_vma=False,
    )
```
